32 devices in a mesh: groups: 2 (over y), ffn: 4 (over x, core), hid: 4 (over z).
Axes of the slice: x: 2, y: 2, z: 4, core: 2. Of those that a mesh axis runs over, the one named last changes fastest.
Arguments:
- inputs: bfloat16 [512, 2, 8192], P(('groups', 'ffn'), None, 'hid'), parts along dimension 0, may hold values from -6 to 6
- gate_weight: bfloat16 [8192, 26624], P('hid', 'ffn'), may hold values from -0.0625 to 0.0625
- up_weight: bfloat16 [8192, 26624], P('hid', 'ffn'), may hold values from -0.0625 to 0.0625
- down_weight: bfloat16 [26624, 8192], P('ffn', 'hid'), may hold values from -0.0390625 to 0.0390625
Outputs:
- outputs: bfloat16 [512, 2, 8192], P(('groups', 'ffn'), None, 'hid'), parts along dimension 0
The draws below stay inside these ranges and needn't reach their ends.
There are 2 independent parts, one for each index of `groups`. The reference program is written for one: setup_inputs(seed, part) draws one part's arguments, and reference() takes and returns one part's arrays. A program takes and returns all parts, laid end to end along the dimension named above; an argument that names none is the same for every part. Nothing has to cross between parts.
All inputs are finite; a program needn't handle non-finite values.
Results may differ from the reference program's by a relative error of at most 0.005.
Values may be sent and summed in bfloat16 or wider, within the bound.
A program may use at most 256 MiB of HBM per device.

```python
import jax
import jax.numpy as jnp

D = 8192
FF = 26624
ROWS = 256
STEPS = 2


def shard_levels(own_key, dims, pieces, least, largest):
    def one(dim, shards_of):
        steps = jax.random.uniform(jax.random.fold_in(jax.random.fold_in(own_key, 6), dim), (shards_of,), jnp.float32, least / len(pieces), largest / len(pieces))
        return jnp.repeat(jnp.exp(steps), dims[dim] // shards_of).reshape((-1,) + (1,) * (len(dims) - dim - 1))

    level = one(*pieces[0])
    for cut in pieces[1:]:
        level = level * one(*cut)
    return level


def bell_draw(own_key, shape, spread, bound, split=(), held_as=jnp.bfloat16):
    entries = jax.random.normal(own_key, shape, jnp.float32) * spread
    if len(split) > 0:
        entries = shard_levels(own_key, shape, split, -0.22, 0.18) * entries
    return jnp.clip(entries, min=-bound, max=bound).astype(held_as)


def setup_inputs(seed: int = 0, part: int = 0) -> dict:
    arg_keys = jax.random.split(jax.random.key(seed), 5)
    part_keys = jax.random.split(jax.random.fold_in(arg_keys[4], part), 5)
    inputs = bell_draw(part_keys[0], (ROWS, STEPS, D), 1.0, 6.0, ((0, 4), (2, 4)))
    gate_weight = bell_draw(arg_keys[1], (D, FF), D ** -0.5, 0.0625, ((0, 4), (1, 4)))
    up_weight = bell_draw(arg_keys[2], (D, FF), D ** -0.5, 0.0625, ((0, 4), (1, 4)))
    down_weight = bell_draw(arg_keys[3], (FF, D), FF ** -0.5, 0.0390625, ((0, 4), (1, 4)))
    return dict(inputs=inputs, gate_weight=gate_weight, up_weight=up_weight, down_weight=down_weight)


def reference(inputs, gate_weight, up_weight, down_weight):
    flat = inputs.reshape(ROWS * STEPS, D)
    gate = jnp.dot(flat, gate_weight, preferred_element_type=jnp.float32)
    up = jnp.dot(flat, up_weight, preferred_element_type=jnp.float32)
    hidden = (jax.nn.silu(gate) * up).astype(jnp.bfloat16)
    mixed = jnp.dot(hidden, down_weight, preferred_element_type=jnp.float32)
    return mixed.astype(jnp.bfloat16).reshape(ROWS, STEPS, D)
```

```python
import functools

import jax
import jax.numpy as jnp
from jax import lax
from jax.experimental import pallas as pl
from jax.experimental.pallas import tpu as pltpu
from jax.sharding import PartitionSpec as P

MESH = pl.DeviceIdType.MESH
GROUPS_OF_ROWS = 2
LAG = 2


def remote(src, dst, send_sem, recv_sem, device_id):
    return pltpu.make_async_remote_copy(
        src_ref=src,
        dst_ref=dst,
        send_sem=send_sem,
        recv_sem=recv_sem,
        device_id=device_id,
        device_id_type=MESH,
    )


def kernel(
    nf, nz, chunk,
    x_ref, wg_ref, wu_ref, wd_ref, out_ref,
    panel, wbuf, dbuf, ring, buf, hid, acc, rs1, snd2, rs2,
    w_sem, d_sem, ps_sem, pr_sem, hs_sem, hr_sem,
    gx_s, gx_r, gc_s, gc_r, c_s, c_r, o_s, o_r,
):
    ng, rg, k = x_ref.shape
    nx = nf // 2
    half = nf // 2
    rows = half * rg
    chunks = wg_ref.shape[1] // chunk
    steps = ng * chunks
    slots = ring.shape[0]

    z = lax.axis_index("hid")
    me = lax.axis_index("ffn")
    x = lax.div(me, 2)
    c = lax.rem(me, 2)
    sibling = {"ffn": 2 * x + 1 - c}

    def ahead(o):
        return lax.rem(x + o, nx)

    def behind(o):
        return lax.rem(x + nx - o, nx)

    def fetch_w(u, action):
        col = pl.ds(pl.multiple_of(lax.rem(u, chunks) * chunk, chunk), chunk)
        slot = lax.rem(u, 2)
        for n, ref in enumerate((wg_ref, wu_ref)):
            action(pltpu.make_async_copy(ref.at[:, col], wbuf.at[slot, n], w_sem.at[slot, n]))

    def fetch_d(way, s, action):
        row = pl.ds(pl.multiple_of(lax.rem(s, chunks) * chunk, chunk), chunk)
        slot = lax.rem(s, 2)
        action(pltpu.make_async_copy(wd_ref.at[row, :], dbuf.at[way, slot], d_sem.at[way, slot]))

    def start(copy):
        copy.start()

    def wait(copy):
        copy.wait()

    fetch_w(jnp.int32(0), start)
    fetch_w(jnp.int32(1), start)

    barrier = pltpu.get_barrier_semaphore()
    pl.semaphore_signal(barrier, inc=1, device_id=sibling, device_id_type=MESH)
    for o in range(1, nx):
        pl.semaphore_signal(
            barrier, inc=1, device_id={"ffn": 2 * ahead(o) + c}, device_id_type=MESH
        )

    @pl.when(z > 0)
    def _():
        pl.semaphore_signal(barrier, inc=1, device_id={"hid": z - 1}, device_id_type=MESH)

    @pl.when(z < nz - 1)
    def _():
        pl.semaphore_signal(barrier, inc=1, device_id={"hid": z + 1}, device_id_type=MESH)

    inner = jnp.where(jnp.logical_and(z > 0, z < nz - 1), 1, 0)
    pl.semaphore_wait(barrier, nx + 1 + inner)

    def to_peer(g, o):
        return remote(
            x_ref.at[g], panel.at[g, me], gx_s.at[g, o], gx_r.at[g, o],
            {"ffn": 2 * ahead(o) + c},
        )

    def from_peer(g, o):
        block = panel.at[g, 2 * behind(o) + c]
        return remote(block, block, gx_s.at[g, o], gx_r.at[g, o], sibling)

    def to_sibling(g, o):
        block = panel.at[g, 2 * behind(o) + c]
        return remote(
            x_ref.at[g] if o == 0 else block, block, gc_s.at[g, o], gc_r.at[g, o], sibling
        )

    def from_sibling(g, o):
        block = panel.at[g, 2 * behind(o) + 1 - c]
        return remote(block, block, gc_s.at[g, o], gc_r.at[g, o], sibling)

    def gather_start(g):
        for o in range(1, nx):
            to_peer(g, o).start()
        to_sibling(g, 0).start()
        panel[g, me] = x_ref[g]

    def gather_forward(g):
        for o in range(1, nx):
            from_peer(g, o).wait_recv()
            to_sibling(g, o).start()

    def gather_end(g):
        for o in range(nx):
            from_sibling(g, o).wait_recv()
        for o in range(1, nx):
            to_peer(g, o).wait_send()
        for o in range(nx):
            to_sibling(g, o).wait_send()

    def to_core(g, p):
        return remote(
            acc.at[g, 2 * p + 1 - c], rs1.at[g, p], c_s.at[g, p], c_r.at[g, p], sibling
        )

    def to_chip(g, o):
        return remote(
            snd2.at[g, o - 1], rs2.at[g, o - 1], o_s.at[g, o], o_r.at[g, o],
            {"ffn": 2 * ahead(o) + c},
        )

    def reduce_start(g):
        for p in range(nx):
            to_core(g, p).start()

    def reduce_middle(g):
        for p in range(nx):
            to_core(g, p).wait_recv()
        for o in range(1, nx):
            p = ahead(o)
            snd2[g, o - 1] = (acc[g, 2 * p + c] + rs1[g, p]).astype(jnp.bfloat16)
            to_chip(g, o).start()

    def reduce_end(g):
        total = acc[g, me] + rs1[g, x]
        for o in range(1, nx):
            to_chip(g, o).wait_recv()
            total = total + rs2[g, o - 1].astype(jnp.float32)
        out_ref[g] = total.astype(jnp.bfloat16)
        for p in range(nx):
            to_core(g, p).wait_send()
        for o in range(1, nx):
            to_chip(g, o).wait_send()

    def project(u):
        g = lax.div(u, chunks)
        slot = lax.rem(u, 2)
        at = lax.rem(u, slots)
        fetch_w(u, wait)
        left = panel[g].reshape(nf * rg, k)
        for n in range(2):
            part = jnp.dot(left, wbuf[slot, n], preferred_element_type=jnp.float32)
            ring[at, 0, :, n * chunk:(n + 1) * chunk] = part[:rows]
            ring[at, 1, :, n * chunk:(n + 1) * chunk] = part[rows:]

    ways = []
    for way in range(2):
        place = z if way == 1 else nz - 1 - z
        sign = 1 if way == 1 else -1
        ways.append((place, {"hid": z + sign}, {"hid": z - sign}))

    def send_sum(way, s, device):
        block = buf.at[way, s]
        return remote(block, block, ps_sem.at[way, s], pr_sem.at[way, s], device)

    def send_hid(way, s, device):
        block = hid.at[way, s]
        return remote(block, block, hs_sem.at[way, s], hr_sem.at[way, s], device)

    def combine(way, t):
        place, onward, back = ways[way]
        s = t - LAG * place

        @pl.when(jnp.logical_and(s >= 0, s < steps))
        def _():
            at = lax.rem(s, slots)

            @pl.when(place == 0)
            def _():
                buf[way, s] = ring[at, way].astype(jnp.bfloat16)
                send_sum(way, s, onward).start()

            @pl.when(jnp.logical_and(place > 0, place < nz - 1))
            def _():
                send_sum(way, s, back).wait_recv()
                buf[way, s] = (buf[way, s].astype(jnp.float32) + ring[at, way]).astype(
                    jnp.bfloat16
                )
                send_sum(way, s, onward).start()

            @pl.when(place == nz - 1)
            def _():
                send_sum(way, s, back).wait_recv()
                total = buf[way, s].astype(jnp.float32) + ring[at, way]
                gate = total[:, :chunk]
                up = total[:, chunk:]
                hid[way, s] = (gate / (1.0 + jnp.exp(-gate)) * up).astype(jnp.bfloat16)
                send_hid(way, s, back).start()

    def step_of(way, t):
        return t - LAG * (2 * (nz - 1) - ways[way][0])

    def forward(way, t):
        place, onward, back = ways[way]
        s = step_of(way, t)

        @pl.when(jnp.logical_and(jnp.logical_and(s >= 0, s < steps), place < nz - 1))
        def _():
            send_hid(way, s, onward).wait_recv()

            @pl.when(place > 0)
            def _():
                send_hid(way, s, back).start()

    def down(way, t):
        s = step_of(way, t)

        @pl.when(jnp.logical_and(s + 1 >= 0, s + 1 < steps))
        def _():
            fetch_d(way, s + 1, start)

        @pl.when(jnp.logical_and(s >= 0, s < steps))
        def _():
            g = lax.div(s, chunks)
            fetch_d(way, s, wait)
            part = jnp.dot(
                hid[way, s], dbuf[way, lax.rem(s, 2)], preferred_element_type=jnp.float32
            )
            blocks = pl.ds(way * half, half)
            acc[g, blocks] += part.reshape(half, rg, part.shape[1])

    gather_start(0)
    acc[...] = jnp.zeros_like(acc)
    gather_forward(0)
    gather_end(0)
    project(jnp.int32(0))

    drain = LAG * 2 * (nz - 1)

    def body(t, carry):
        for way in range(2):
            combine(way, t)
        for way in range(2):
            forward(way, t)

        @pl.when(t + 2 < steps)
        def _():
            fetch_w(t + 2, start)

        for g in range(1, ng):
            @pl.when(t == (g - 1) * chunks + 2)
            def _():
                gather_start(g)

            @pl.when(t == g * chunks - 3)
            def _():
                gather_forward(g)

            @pl.when(t == g * chunks - 1)
            def _():
                gather_end(g)

        @pl.when(t + 1 < steps)
        def _():
            project(t + 1)

        for way in range(2):
            down(way, t)

        for g in range(ng - 1):
            done = (g + 1) * chunks - 1 + drain

            @pl.when(t == done)
            def _():
                reduce_start(g)

            @pl.when(t == done + 2)
            def _():
                reduce_middle(g)

            @pl.when(t == done + 5)
            def _():
                reduce_end(g)

        return carry

    lax.fori_loop(0, steps + drain, body, 0)

    last = ng - 1
    reduce_start(last)
    reduce_middle(last)
    reduce_end(last)

    def finish(s, carry):
        for way in range(2):
            place, onward, back = ways[way]

            @pl.when(place < nz - 1)
            def _():
                send_sum(way, s, onward).wait_send()

            @pl.when(place > 0)
            def _():
                send_hid(way, s, back).wait_send()

        return carry

    lax.fori_loop(0, steps, finish, 0)


def per_device(nf, nz, inputs, gate_weight, up_weight, down_weight):
    ng = GROUPS_OF_ROWS
    k = inputs.shape[2]
    block = inputs.shape[0] * inputs.shape[1]
    rg = block // ng
    nx = nf // 2
    rows = nx * rg
    units = gate_weight.shape[1]
    chunk = 256 if units % 256 == 0 else 128
    steps = ng * (units // chunk)
    slots = LAG * (nz - 1) + 1
    wide = down_weight.shape[1]
    bf16, f32 = jnp.bfloat16, jnp.float32
    dma = pltpu.SemaphoreType.DMA
    peers = max(nx - 1, 1)
    result = pl.pallas_call(
        functools.partial(kernel, nf, nz, chunk),
        out_shape=jax.ShapeDtypeStruct((ng, rg, wide), bf16),
        in_specs=[pl.BlockSpec(memory_space=pltpu.VMEM)]
        + [pl.BlockSpec(memory_space=pl.ANY)] * 3,
        out_specs=pl.BlockSpec(memory_space=pltpu.VMEM),
        scratch_shapes=[
            pltpu.VMEM((ng, nf, rg, k), bf16),
            pltpu.VMEM((2, 2, k, chunk), bf16),
            pltpu.VMEM((2, 2, chunk, wide), bf16),
            pltpu.VMEM((slots, 2, rows, 2 * chunk), f32),
            pltpu.VMEM((2, steps, rows, 2 * chunk), bf16),
            pltpu.VMEM((2, steps, rows, chunk), bf16),
            pltpu.VMEM((ng, nf, rg, wide), f32),
            pltpu.VMEM((ng, nx, rg, wide), f32),
            pltpu.VMEM((ng, peers, rg, wide), bf16),
            pltpu.VMEM((ng, peers, rg, wide), bf16),
            dma((2, 2)),
            dma((2, 2)),
            dma((2, steps)),
            dma((2, steps)),
            dma((2, steps)),
            dma((2, steps)),
            dma((ng, nx)),
            dma((ng, nx)),
            dma((ng, nx)),
            dma((ng, nx)),
            dma((ng, nx)),
            dma((ng, nx)),
            dma((ng, nx)),
            dma((ng, nx)),
        ],
        compiler_params=pltpu.CompilerParams(
            collective_id=0, has_side_effects=True, vmem_limit_bytes=60 * 1024 * 1024
        ),
    )(inputs.reshape(ng, rg, k), gate_weight, up_weight, down_weight)
    return result.reshape(inputs.shape[0], inputs.shape[1], wide)


def solution(mesh):
    return jax.shard_map(
        functools.partial(per_device, mesh.shape["ffn"], mesh.shape["hid"]),
        mesh=mesh,
        in_specs=(
            P(("groups", "ffn"), None, "hid"),
            P("hid", "ffn"),
            P("hid", "ffn"),
            P("ffn", "hid"),
        ),
        out_specs=P(("groups", "ffn"), None, "hid"),
        check_vma=False,
    )
```

```python
import functools

import jax
import jax.numpy as jnp
from jax import lax
from jax.experimental import pallas as pl
from jax.experimental.pallas import tpu as pltpu
from jax.sharding import PartitionSpec as P

MESH = pl.DeviceIdType.MESH
GROUPS_OF_ROWS = 2
LAG = 1


def remote(src, dst, send_sem, recv_sem, device_id):
    return pltpu.make_async_remote_copy(
        src_ref=src,
        dst_ref=dst,
        send_sem=send_sem,
        recv_sem=recv_sem,
        device_id=device_id,
        device_id_type=MESH,
    )


def kernel(
    nf, nz, chunk,
    x_ref, wg_ref, wu_ref, wd_ref, out_ref,
    panel, wbuf, dbuf, ring, buf, hid, acc, rs1, snd2, rs2,
    w_sem, d_sem, ps_sem, pr_sem, hs_sem, hr_sem,
    gx_s, gx_r, gc_s, gc_r, c_s, c_r, o_s, o_r,
):
    ng, rg, k = x_ref.shape
    nx = nf // 2
    half = nf // 2
    rows = half * rg
    chunks = wg_ref.shape[1] // chunk
    steps = ng * chunks
    slots = ring.shape[0]

    z = lax.axis_index("hid")
    me = lax.axis_index("ffn")
    x = lax.div(me, 2)
    c = lax.rem(me, 2)
    sibling = {"ffn": 2 * x + 1 - c}

    def ahead(o):
        return lax.rem(x + o, nx)

    def behind(o):
        return lax.rem(x + nx - o, nx)

    def fetch_w(u, action):
        col = pl.ds(pl.multiple_of(lax.rem(u, chunks) * chunk, chunk), chunk)
        slot = lax.rem(u, 2)
        for n, ref in enumerate((wg_ref, wu_ref)):
            action(pltpu.make_async_copy(ref.at[:, col], wbuf.at[slot, n], w_sem.at[slot, n]))

    def fetch_d(way, s, action):
        row = pl.ds(pl.multiple_of(lax.rem(s, chunks) * chunk, chunk), chunk)
        slot = lax.rem(s, 2)
        action(pltpu.make_async_copy(wd_ref.at[row, :], dbuf.at[way, slot], d_sem.at[way, slot]))

    def start(copy):
        copy.start()

    def wait(copy):
        copy.wait()

    fetch_w(jnp.int32(0), start)
    fetch_w(jnp.int32(1), start)

    barrier = pltpu.get_barrier_semaphore()
    pl.semaphore_signal(barrier, inc=1, device_id=sibling, device_id_type=MESH)
    for o in range(1, nx):
        pl.semaphore_signal(
            barrier, inc=1, device_id={"ffn": 2 * ahead(o) + c}, device_id_type=MESH
        )

    @pl.when(z > 0)
    def _():
        pl.semaphore_signal(barrier, inc=1, device_id={"hid": z - 1}, device_id_type=MESH)

    @pl.when(z < nz - 1)
    def _():
        pl.semaphore_signal(barrier, inc=1, device_id={"hid": z + 1}, device_id_type=MESH)

    inner = jnp.where(jnp.logical_and(z > 0, z < nz - 1), 1, 0)
    pl.semaphore_wait(barrier, nx + 1 + inner)

    def to_peer(g, o):
        return remote(
            x_ref.at[g], panel.at[g, me], gx_s.at[g, o], gx_r.at[g, o],
            {"ffn": 2 * ahead(o) + c},
        )

    def from_peer(g, o):
        block = panel.at[g, 2 * behind(o) + c]
        return remote(block, block, gx_s.at[g, o], gx_r.at[g, o], sibling)

    def to_sibling(g, o):
        block = panel.at[g, 2 * behind(o) + c]
        return remote(
            x_ref.at[g] if o == 0 else block, block, gc_s.at[g, o], gc_r.at[g, o], sibling
        )

    def from_sibling(g, o):
        block = panel.at[g, 2 * behind(o) + 1 - c]
        return remote(block, block, gc_s.at[g, o], gc_r.at[g, o], sibling)

    def gather_start(g):
        for o in range(1, nx):
            to_peer(g, o).start()
        to_sibling(g, 0).start()
        panel[g, me] = x_ref[g]

    def gather_forward(g):
        for o in range(1, nx):
            from_peer(g, o).wait_recv()
            to_sibling(g, o).start()

    def gather_end(g):
        for o in range(nx):
            from_sibling(g, o).wait_recv()
        for o in range(1, nx):
            to_peer(g, o).wait_send()
        for o in range(nx):
            to_sibling(g, o).wait_send()

    def to_core(g, p):
        return remote(
            acc.at[g, 2 * p + 1 - c], rs1.at[g, p], c_s.at[g, p], c_r.at[g, p], sibling
        )

    def to_chip(g, o):
        return remote(
            snd2.at[g, o - 1], rs2.at[g, o - 1], o_s.at[g, o], o_r.at[g, o],
            {"ffn": 2 * ahead(o) + c},
        )

    def reduce_start(g):
        for p in range(nx):
            to_core(g, p).start()

    def reduce_middle(g):
        for p in range(nx):
            to_core(g, p).wait_recv()
        for o in range(1, nx):
            p = ahead(o)
            snd2[g, o - 1] = (acc[g, 2 * p + c] + rs1[g, p]).astype(jnp.bfloat16)
            to_chip(g, o).start()

    def reduce_end(g):
        total = acc[g, me] + rs1[g, x]
        for o in range(1, nx):
            to_chip(g, o).wait_recv()
            total = total + rs2[g, o - 1].astype(jnp.float32)
        out_ref[g] = total.astype(jnp.bfloat16)
        for p in range(nx):
            to_core(g, p).wait_send()
        for o in range(1, nx):
            to_chip(g, o).wait_send()

    def project(u):
        g = lax.div(u, chunks)
        slot = lax.rem(u, 2)
        at = lax.rem(u, slots)
        fetch_w(u, wait)
        left = panel[g].reshape(nf * rg, k)
        for n in range(2):
            part = jnp.dot(left, wbuf[slot, n], preferred_element_type=jnp.float32)
            ring[at, 0, :, n * chunk:(n + 1) * chunk] = part[:rows]
            ring[at, 1, :, n * chunk:(n + 1) * chunk] = part[rows:]

    ways = []
    for way in range(2):
        place = z if way == 1 else nz - 1 - z
        sign = 1 if way == 1 else -1
        ways.append((place, {"hid": z + sign}, {"hid": z - sign}))

    def send_sum(way, s, device):
        block = buf.at[way, s]
        return remote(block, block, ps_sem.at[way, s], pr_sem.at[way, s], device)

    def send_hid(way, s, device):
        block = hid.at[way, s]
        return remote(block, block, hs_sem.at[way, s], hr_sem.at[way, s], device)

    def combine(way, t):
        place, onward, back = ways[way]
        s = t - LAG * place

        @pl.when(jnp.logical_and(s >= 0, s < steps))
        def _():
            at = lax.rem(s, slots)

            @pl.when(place == 0)
            def _():
                buf[way, s] = ring[at, way].astype(jnp.bfloat16)
                send_sum(way, s, onward).start()

            @pl.when(jnp.logical_and(place > 0, place < nz - 1))
            def _():
                send_sum(way, s, back).wait_recv()
                buf[way, s] = (buf[way, s].astype(jnp.float32) + ring[at, way]).astype(
                    jnp.bfloat16
                )
                send_sum(way, s, onward).start()

            @pl.when(place == nz - 1)
            def _():
                send_sum(way, s, back).wait_recv()
                total = buf[way, s].astype(jnp.float32) + ring[at, way]
                gate = total[:, :chunk]
                up = total[:, chunk:]
                hid[way, s] = (gate / (1.0 + jnp.exp(-gate)) * up).astype(jnp.bfloat16)
                send_hid(way, s, back).start()

    def step_of(way, t):
        return t - LAG * (2 * (nz - 1) - ways[way][0])

    def forward(way, t):
        place, onward, back = ways[way]
        s = step_of(way, t)

        @pl.when(jnp.logical_and(jnp.logical_and(s >= 0, s < steps), place < nz - 1))
        def _():
            send_hid(way, s, onward).wait_recv()

            @pl.when(place > 0)
            def _():
                send_hid(way, s, back).start()

    def down(way, t):
        s = step_of(way, t)

        @pl.when(jnp.logical_and(s + 1 >= 0, s + 1 < steps))
        def _():
            fetch_d(way, s + 1, start)

        @pl.when(jnp.logical_and(s >= 0, s < steps))
        def _():
            g = lax.div(s, chunks)
            fetch_d(way, s, wait)
            part = jnp.dot(
                hid[way, s], dbuf[way, lax.rem(s, 2)], preferred_element_type=jnp.float32
            )
            blocks = pl.ds(way * half, half)
            acc[g, blocks] += part.reshape(half, rg, part.shape[1])

    gather_start(0)
    acc[...] = jnp.zeros_like(acc)
    gather_forward(0)
    gather_end(0)
    project(jnp.int32(0))

    drain = LAG * 2 * (nz - 1)

    def body(t, carry):
        for way in range(2):
            combine(way, t)
        for way in range(2):
            forward(way, t)

        @pl.when(t + 2 < steps)
        def _():
            fetch_w(t + 2, start)

        for g in range(1, ng):
            @pl.when(t == (g - 1) * chunks + 2)
            def _():
                gather_start(g)

            @pl.when(t == g * chunks - 3)
            def _():
                gather_forward(g)

            @pl.when(t == g * chunks - 1)
            def _():
                gather_end(g)

        @pl.when(t + 1 < steps)
        def _():
            project(t + 1)

        for way in range(2):
            down(way, t)

        for g in range(ng - 1):
            done = (g + 1) * chunks - 1 + drain

            @pl.when(t == done)
            def _():
                reduce_start(g)

            @pl.when(t == done + 2)
            def _():
                reduce_middle(g)

            @pl.when(t == done + 5)
            def _():
                reduce_end(g)

        return carry

    lax.fori_loop(0, steps + drain, body, 0)

    last = ng - 1
    reduce_start(last)
    reduce_middle(last)
    reduce_end(last)

    def finish(s, carry):
        for way in range(2):
            place, onward, back = ways[way]

            @pl.when(place < nz - 1)
            def _():
                send_sum(way, s, onward).wait_send()

            @pl.when(place > 0)
            def _():
                send_hid(way, s, back).wait_send()

        return carry

    lax.fori_loop(0, steps, finish, 0)


def per_device(nf, nz, inputs, gate_weight, up_weight, down_weight):
    ng = GROUPS_OF_ROWS
    k = inputs.shape[2]
    block = inputs.shape[0] * inputs.shape[1]
    rg = block // ng
    nx = nf // 2
    rows = nx * rg
    units = gate_weight.shape[1]
    chunk = 256 if units % 256 == 0 else 128
    steps = ng * (units // chunk)
    slots = LAG * (nz - 1) + 1
    wide = down_weight.shape[1]
    bf16, f32 = jnp.bfloat16, jnp.float32
    dma = pltpu.SemaphoreType.DMA
    peers = max(nx - 1, 1)
    result = pl.pallas_call(
        functools.partial(kernel, nf, nz, chunk),
        out_shape=jax.ShapeDtypeStruct((ng, rg, wide), bf16),
        in_specs=[pl.BlockSpec(memory_space=pltpu.VMEM)]
        + [pl.BlockSpec(memory_space=pl.ANY)] * 3,
        out_specs=pl.BlockSpec(memory_space=pltpu.VMEM),
        scratch_shapes=[
            pltpu.VMEM((ng, nf, rg, k), bf16),
            pltpu.VMEM((2, 2, k, chunk), bf16),
            pltpu.VMEM((2, 2, chunk, wide), bf16),
            pltpu.VMEM((slots, 2, rows, 2 * chunk), f32),
            pltpu.VMEM((2, steps, rows, 2 * chunk), bf16),
            pltpu.VMEM((2, steps, rows, chunk), bf16),
            pltpu.VMEM((ng, nf, rg, wide), f32),
            pltpu.VMEM((ng, nx, rg, wide), f32),
            pltpu.VMEM((ng, peers, rg, wide), bf16),
            pltpu.VMEM((ng, peers, rg, wide), bf16),
            dma((2, 2)),
            dma((2, 2)),
            dma((2, steps)),
            dma((2, steps)),
            dma((2, steps)),
            dma((2, steps)),
            dma((ng, nx)),
            dma((ng, nx)),
            dma((ng, nx)),
            dma((ng, nx)),
            dma((ng, nx)),
            dma((ng, nx)),
            dma((ng, nx)),
            dma((ng, nx)),
        ],
        compiler_params=pltpu.CompilerParams(
            collective_id=0, has_side_effects=True, vmem_limit_bytes=60 * 1024 * 1024
        ),
    )(inputs.reshape(ng, rg, k), gate_weight, up_weight, down_weight)
    return result.reshape(inputs.shape[0], inputs.shape[1], wide)


def solution(mesh):
    return jax.shard_map(
        functools.partial(per_device, mesh.shape["ffn"], mesh.shape["hid"]),
        mesh=mesh,
        in_specs=(
            P(("groups", "ffn"), None, "hid"),
            P("hid", "ffn"),
            P("hid", "ffn"),
            P("ffn", "hid"),
        ),
        out_specs=P(("groups", "ffn"), None, "hid"),
        check_vma=False,
    )
```
